128 devices in a mesh: dp: 16 (over x, y_hi, core), pipe: 8 (over z, y_lo).
Axes of the slice: x: 4, y: 4 (y_hi: 2, y_lo: 2; y = y_hi * 2 + y_lo), z: 4, core: 2. Of those that a mesh axis runs over, the one named last changes fastest.
Arguments:
- tokens_in: bfloat16 [8, 2, 2048, 6144], P('pipe', None, 'dp'), may hold values from -6 to 6
- grad_first: bfloat16 [8, 2048, 6144], P('pipe', 'dp'), may hold values from -6 to 6
- grad_last: bfloat16 [2048, 6144], P('dp'), may hold values from -6 to 6
- expert_ids: int32 [8, 2, 2048, 1], P('pipe', None, 'dp'), may hold values from 0 to 1
- gate_probs: float32 [8, 2, 2048], P('pipe', None, 'dp'), may hold values from 0.2 to 1
- w_gate: bfloat16 [8, 2, 6144, 256], P('pipe', None, 'dp'), may hold values from -0.078125 to 0.078125
- w_up: bfloat16 [8, 2, 6144, 256], P('pipe', None, 'dp'), may hold values from -0.078125 to 0.078125
- w_down: bfloat16 [8, 2, 256, 6144], P('pipe', None, None, 'dp'), may hold values from -0.375 to 0.375
Outputs:
- grad_back: bfloat16 [8, 2048, 6144], P('pipe', 'dp')
- d_gate: float32 [8, 2, 6144, 256], P('pipe', None, 'dp')
- d_up: float32 [8, 2, 6144, 256], P('pipe', None, 'dp')
- d_down: float32 [8, 2, 256, 6144], P('pipe', None, None, 'dp')
The draws below stay inside these ranges and needn't reach their ends.
Inputs may be any that keep to these rules, and one draw needn't show every extreme that they name: `expert_ids`: each token names one expert; every expert is named by some token.
All inputs are finite; a program needn't handle non-finite values.
Results may differ from the reference program's by a relative error of at most 0.017.
Values may be sent and summed in bfloat16 or wider, within the bound.
A program may use at most 192 MiB of HBM per device.

```python
import math
import jax
import jax.numpy as jnp
from jax import lax

D = 6144
FF_R = 256
EXP = 2
MB = 2
TOK_DEV = 128
TOKENS = 2048
N_DP = 16
N_PIPE = 8


def strengthened(drawn, key, source, target, parts, factor):
    def block_of(axis_at):
        return (jnp.arange(drawn.shape[axis_at]) // (drawn.shape[axis_at] // parts)).reshape((-1,) + (1,) * (drawn.ndim - 1 - axis_at))

    near = jax.random.permutation(key, parts)[block_of(target)]
    far = (block_of(target) + parts // 2) % parts
    return jnp.where((block_of(source) == near) | (block_of(source) == far), factor * drawn, drawn)


def block_levels(own_key, shape, split, smallest, high):
    factor_of, own = 1.0, jax.random.fold_in(own_key, 6)
    for position, shards_of in split:
        steps = jnp.exp(jax.random.uniform(jax.random.fold_in(own, position), (shards_of,), jnp.float32, smallest / len(split), high / len(split)))
        factor_of = factor_of * jnp.repeat(steps, shape[position] // shards_of).reshape([-1 if axis == position else 1 for axis in range(len(shape))])
    return factor_of


def different_ones(stream_key, rows, count, top, lift):
    ranking = jax.random.permutation(jax.random.fold_in(stream_key, 1), count)
    boost = ranking
    for power in range(3):
        boost = boost * boost // count
    boost = boost * lift // count
    chance = jax.random.randint(jax.random.fold_in(stream_key, 2), (rows, count), 0, 4096) + boost
    sure = jax.random.permutation(jax.random.fold_in(stream_key, 3), rows)[jnp.arange(count) % rows]
    chance = jnp.where(jnp.arange(rows)[:, None] == sure[None, :], 1 << 14, chance)
    merit = chance * count + jnp.arange(count)
    return lax.top_k(merit.astype(jnp.int32), top)[1].astype(jnp.int32)


def gaussian(key, dims, deviation, bound, split=(), dtype=jnp.bfloat16):
    entries = deviation * jax.random.normal(key, dims, jnp.float32)
    if split:
        entries = entries * block_levels(key, dims, split, -0.22, 0.18)
    return jnp.clip(entries, -bound, bound).astype(dtype)


def bell_draw_with(key, shape, deviation, reach, split, heavy, kind=jnp.bfloat16):
    drawn = deviation * jax.random.normal(key, shape, jnp.float32)
    if split:
        drawn = drawn * block_levels(key, shape, split, -0.22, 0.18)
    return jnp.clip(strengthened(drawn, jax.random.fold_in(key, 3), *heavy), -reach, reach).astype(kind)


def setup_inputs(seed: int = 0) -> dict:
    keys = jax.random.split(jax.random.key(seed), 9)
    return {
        "tokens_in": gaussian(keys[0], (N_PIPE, MB, TOKENS, D), 1.0, 6.0, ((0, 8), (2, 16))),
        "grad_first": bell_draw_with(keys[1], (N_PIPE, TOKENS, D), 1.0, 6.0, ((0, 8), (1, 16)), (1, 2, 16, 2.0)),
        "grad_last": gaussian(keys[2], (TOKENS, D), 1.0, 6.0, ((0, 16),)),
        "expert_ids": different_ones(keys[3], N_PIPE * MB * TOKENS, EXP, 1, 8192).reshape((N_PIPE, MB, TOKENS, 1)),
        "gate_probs": jnp.clip(0.2 + 0.8 * jax.random.uniform(keys[4], (N_PIPE, MB, TOKENS), jnp.float32) ** block_levels(keys[4], (N_PIPE, MB, TOKENS), ((0, 8), (2, 16)), -0.2, 0.2), 0.2, 1.0),
        "w_gate": gaussian(keys[5], (N_PIPE, EXP, D, FF_R), D ** -0.5, 0.078125, ((0, 8), (2, 16))),
        "w_up": gaussian(keys[6], (N_PIPE, EXP, D, FF_R), D ** -0.5, 0.078125, ((0, 8), (2, 16))),
        "w_down": gaussian(keys[7], (N_PIPE, EXP, FF_R, D), FF_R ** -0.5, 0.375, ((0, 8), (3, 16))),
    }


def activations(pre_gate, pre_up, down_grad):
    sigmoid_gate = jax.nn.sigmoid(pre_gate)
    silu_gate = pre_gate * sigmoid_gate
    grad_gate = (down_grad * pre_up * sigmoid_gate * (1.0 + pre_gate * (1.0 - sigmoid_gate))).astype(jnp.bfloat16)
    grad_up = (down_grad * silu_gate).astype(jnp.bfloat16)
    return (silu_gate * pre_up, grad_gate, grad_up)

def matmul(left, right, form):
    return jnp.einsum(form, left.astype(jnp.float32), right.astype(jnp.float32), precision=lax.Precision.HIGHEST)

def section_pass(rows_in, rows_grad, expert_of, gates, gate_proj, up_proj, down_proj):
    input_grad = jnp.zeros(rows_in.shape, jnp.float32)
    gate_parts = []
    up_parts = []
    down_parts = []
    for expert in range(EXP):
        row_weight = jnp.where(expert_of == expert, gates, jnp.float32(0.0))[:, None]
        pre_gate = matmul(rows_in, gate_proj[expert], 'td,df->tf')
        pre_up = matmul(rows_in, up_proj[expert], 'td,df->tf')
        down_grad = row_weight * matmul(rows_grad, down_proj[expert], 'td,fd->tf')
        hidden, grad_gate, grad_up = activations(pre_gate, pre_up, down_grad)
        scaled_hidden = (row_weight * hidden).astype(jnp.bfloat16)
        input_grad = input_grad + matmul(grad_gate, gate_proj[expert], 'tf,df->td') + matmul(grad_up, up_proj[expert], 'tf,df->td')
        split_in = rows_in.reshape(N_DP, TOK_DEV, D)
        split_grad = rows_grad.reshape(N_DP, TOK_DEV, D)
        gate_parts.append(matmul(split_in, grad_gate.reshape(N_DP, TOK_DEV, FF_R), 'rtd,rtf->rdf'))
        up_parts.append(matmul(split_in, grad_up.reshape(N_DP, TOK_DEV, FF_R), 'rtd,rtf->rdf'))
        down_parts.append(matmul(scaled_hidden.reshape(N_DP, TOK_DEV, FF_R), split_grad, 'rtf,rtd->rfd'))
    return (input_grad, (jnp.stack(gate_parts, 1), jnp.stack(up_parts, 1), jnp.stack(down_parts, 1)))

def owner_sum(first_part, second_part, grad_scale):
    rounded = ((first_part + second_part) * grad_scale).astype(jnp.bfloat16)
    rounded = lax.optimization_barrier(rounded)
    return lax.optimization_barrier(jnp.sum(rounded.astype(jnp.float32), 0))

def reference(tokens_in, grad_first, grad_last, expert_ids, gate_probs, w_gate, w_up, w_down):
    grad_scale = 1.0 / math.sqrt(TOKENS)
    backs = [None] * N_PIPE
    gate_out = [None] * N_PIPE
    up_out = [None] * N_PIPE
    down_out = [None] * N_PIPE
    arrived = grad_last
    for section_index in reversed(range(N_PIPE)):
        first_grad, first_parts = section_pass(tokens_in[section_index, 0], grad_first[section_index], expert_ids[section_index, 0, :, 0], gate_probs[section_index, 0], w_gate[section_index], w_up[section_index], w_down[section_index])
        sent = (grad_first[section_index].astype(jnp.float32) + first_grad).astype(jnp.bfloat16)
        second_dy = arrived
        second_grad, second_parts = section_pass(tokens_in[section_index, 1], second_dy, expert_ids[section_index, 1, :, 0], gate_probs[section_index, 1], w_gate[section_index], w_up[section_index], w_down[section_index])
        backs[section_index] = (second_dy.astype(jnp.float32) + second_grad).astype(jnp.bfloat16)
        gate_out[section_index] = owner_sum(first_parts[0], second_parts[0], grad_scale)
        up_out[section_index] = owner_sum(first_parts[1], second_parts[1], grad_scale)
        down_out[section_index] = owner_sum(first_parts[2], second_parts[2], grad_scale)
        arrived = sent
    return (jnp.stack(backs), jnp.stack(gate_out), jnp.stack(up_out), jnp.stack(down_out))
```

```python
import functools
import math

import jax
import jax.numpy as jnp
from jax import lax
from jax.experimental import pallas as pl
from jax.experimental.pallas import tpu as pltpu
from jax.sharding import PartitionSpec as P

MESH = pl.DeviceIdType.MESH
BF = jnp.bfloat16
F32 = jnp.float32

NX = 4
CHUNKS = 2


def dot(a, b):
    return lax.dot_general(a, b, (((1,), (0,)), ((), ())), preferred_element_type=F32)


def dot_t(a, b):
    return lax.dot_general(a, b, (((1,), (1,)), ((), ())), preferred_element_type=F32)


class Sems:
    def __init__(self):
        self.count = 0
        self.index = {}

    def __call__(self, *key):
        if key not in self.index:
            self.index[key] = self.count
            self.count += 1
        return self.index[key]


def kernel(
    dims, tok, n_sems,
    x_ref, g1_ref, gl_ref, meta_ref, wg_ref, wu_ref, wd_ref,
    back_ref, dg_ref, du_ref, dd_ref,
    xs, gs, sent, bk, wgu, wdn, metas, msk, prob, xt, sht, act, amask, shm,
    p1gu, r1gu, owngu, s2gu, r2gu, p1d, r1d, ownd, s2d, r2d,
    accgu, accd, pgu, pd, qgu, qd, sem,
):
    wide, half, hid = dims
    n_ch = CHUNKS
    tk = tok // n_ch
    rows = 2 * NX * tk
    four = NX * tk
    tile = min(256, four)
    scale = 1.0 / math.sqrt(tok * lax.axis_size("dp"))

    dp = lax.axis_index("dp")
    sec = lax.axis_index("pipe")
    n_sec = lax.axis_size("pipe")
    x = lax.div(dp, 4)
    yh = lax.rem(lax.div(dp, 2), 2)
    c = lax.rem(dp, 2)
    oc = 1 - c
    block = c * NX + x

    def member(dx, dc):
        px = lax.rem(x + dx, NX)
        pc = lax.rem(c + dc, 2)
        return px, pc, (px * 4 + yh * 2 + pc, sec)

    core_peer = (x * 4 + yh * 2 + oc, sec)
    y_peer = (x * 4 + (1 - yh) * 2 + c, sec)
    before = (dp, lax.rem(sec + n_sec - 1, n_sec))
    after = (dp, lax.rem(sec + 1, n_sec))
    offsets = [(1, 0), (3, 0), (1, 1), (3, 1), (2, 0), (2, 1), (0, 1)]

    names = Sems()
    sends = []

    def s_at(*key):
        return sem.at[names(*key)]

    def rdma(src, dst, ssem, rsem, device):
        pltpu.make_async_remote_copy(
            src_ref=src, dst_ref=dst, send_sem=ssem, recv_sem=rsem,
            device_id=device, device_id_type=MESH,
        ).start()

    def drain(ref, s):
        pltpu.make_async_copy(ref, ref, s).wait()

    def cols_of(px, pc, h):
        return pl.multiple_of(half * (px * 4 + lax.rem(yh + h, 2) * 2 + pc), 128)

    def at(start, size):
        return pl.ds(pl.multiple_of(start, 16), size)

    bar = pltpu.get_barrier_semaphore()
    for dx, dc in offsets:
        pl.semaphore_signal(bar, inc=1, device_id=member(dx, dc)[2], device_id_type=MESH)
    pl.semaphore_signal(bar, inc=1, device_id=y_peer, device_id_type=MESH)
    pl.semaphore_signal(bar, inc=1, device_id=after, device_id_type=MESH)
    pl.semaphore_wait(bar, len(offsets) + 2)

    def spread_meta():
        ss, rs = s_at("meta", "s"), s_at("meta", "r")
        for dx, dc in offsets:
            rdma(meta_ref, metas.at[block], ss, rs, member(dx, dc)[2])
        pltpu.make_async_copy(meta_ref, metas.at[block], rs).start()
        sends.append((ss, metas.at[pl.ds(0, len(offsets))]))

    def masks():
        drain(metas, s_at("meta", "r"))
        for mb in range(2):
            for b in range(2 * NX):
                row = metas[b, mb : mb + 1, :]
                col = jnp.transpose(jnp.broadcast_to(row, (128, 128)))
                for k in range(n_ch):
                    msk[mb, k, b * tk : (b + 1) * tk, :] = col[k * tk : (k + 1) * tk, :]
            row = meta_ref[2 + mb : 3 + mb, :]
            prob[mb] = jnp.transpose(jnp.broadcast_to(row, (128, 128)))

    def weights():
        ss, rs = s_at("wgu", "s"), s_at("wgu", "r")
        for j, (ref, e) in enumerate([(wg_ref, 0), (wg_ref, 1), (wu_ref, 0), (wu_ref, 1)]):
            src = ref.at[0, e]
            cs = pl.ds(j * hid, hid)
            rdma(src, wgu.at[pl.ds(half, half), cs], ss, rs, y_peer)
            pltpu.make_async_copy(src, wgu.at[pl.ds(0, half), cs], rs).start()
        sends.append((ss, wgu.at[pl.ds(0, half)]))
        ss, rs = s_at("wd", "s"), s_at("wd", "r")
        for e in range(2):
            src = wd_ref.at[0, e]
            rr = pl.ds(e * hid, hid)
            rdma(src, wdn.at[rr, pl.ds(half, half)], ss, rs, y_peer)
            pltpu.make_async_copy(src, wdn.at[rr, pl.ds(0, half)], rs).start()
        sends.append((ss, wdn.at[:, pl.ds(0, half)]))

    def spread(src, dst, k, ss, rs):
        for dx, dc in offsets + [(0, 0)]:
            px, pc, device = member(dx, dc)
            for h in range(2):
                a = src.at[pl.ds(k * tk, tk), pl.ds(cols_of(px, pc, h), half)]
                b = dst.at[at(block * tk, tk), pl.ds(h * half, half)]
                if (dx, dc) == (0, 0):
                    pltpu.make_async_copy(a, b, rs).start()
                else:
                    rdma(a, b, ss, rs, device)

    def spread_x(mb, k):
        ss = s_at("x", mb, k, "s")
        spread(x_ref.at[0, mb], xs.at[mb, k], k, ss, s_at("x", mb, k, "r"))
        sends.append((ss, xs.at[mb, k, pl.ds(0, rows - tk)]))

    def spread_g(k):
        ss = s_at("g", 0, k, "s")
        spread(g1_ref.at[0], gs.at[0, k], k, ss, s_at("g", 0, k, "r"))
        sends.append((ss, gs.at[0, k, pl.ds(0, rows - tk)]))

    def spread_last(k):
        @pl.when(sec == n_sec - 1)
        def _():
            spread(gl_ref, gs.at[1, k], k, s_at("last", k, "s"), s_at("g", 1, k, "r"))

    def wait_x(mb, k):
        drain(xs.at[mb, k], s_at("x", mb, k, "r"))

    def wait_g(mb, k):
        drain(gs.at[mb, k], s_at("g", mb, k, "r"))

    def wide_mask(mb, k, start, size):
        m = msk[mb, k, at(start, size), :]
        return jnp.concatenate([m] * (hid // 128), axis=1)

    def pre_gu(mb, k):
        def step(base, out, out_base, kind):
            def one(i, carry):
                r = base + i * tile
                lhs = xs[mb, k, at(r, tile), :]
                second = wide_mask(mb, k, r, tile) != 0.0
                for part in range(2):
                    res = dot(lhs, wgu[:, part * 2 * hid : (part + 1) * 2 * hid])
                    pick = jnp.where(second, res[:, hid:], res[:, :hid])
                    out[mb, k, at(out_base + i * tile, tile), part * hid : (part + 1) * hid] = pick.astype(kind)
                return carry

            lax.fori_loop(0, four // tile, one, 0)

        step(oc * four, p1gu, 0, BF)
        ss = s_at("p1gu", mb, k, "s")
        rdma(p1gu.at[mb, k], r1gu.at[mb, k], ss, s_at("p1gu", mb, k, "r"), core_peer)
        sends.append((ss, p1gu.at[mb, k]))
        step(c * four, owngu, 0, F32)

    def pre_d(mb, k):
        def step(base, out, kind):
            def one(i, carry):
                r = base + i * tile
                res = dot_t(gs[mb, k, at(r, tile), :], wdn[...])
                second = wide_mask(mb, k, r, tile) != 0.0
                pick = jnp.where(second, res[:, hid:], res[:, :hid])
                out[mb, k, at(i * tile, tile), :] = pick.astype(kind)
                return carry

            lax.fori_loop(0, four // tile, one, 0)

        step(oc * four, p1d, BF)
        ss = s_at("p1d", mb, k, "s")
        rdma(p1d.at[mb, k], r1d.at[mb, k], ss, s_at("p1d", mb, k, "r"), core_peer)
        sends.append((ss, p1d.at[mb, k]))
        step(c * four, ownd, F32)

    def along_x(tag, own, r1, s2, r2, mb, k):
        drain(r1.at[mb, k], s_at("p1" + tag, mb, k, "r"))
        ss, rs = s_at("s2" + tag, mb, k, "s"), s_at("s2" + tag, mb, k, "r")
        for dx in (2, 1, 3):
            px, _, device = member(dx, 0)
            rr = at(px * tk, tk)
            s2[mb, k, dx - 1] = (own[mb, k, rr, :] + r1[mb, k, rr, :].astype(F32)).astype(BF)
            rdma(s2.at[mb, k, dx - 1], r2.at[mb, k, dx - 1], ss, rs, device)
        sends.append((ss, s2.at[mb, k]))

    def mid_gu(mb, k):
        along_x("gu", owngu, r1gu, s2gu, r2gu, mb, k)

    def mid_d(mb, k):
        along_x("d", ownd, r1d, s2d, r2d, mb, k)

    def total(tag, own, r1, r2, mb, k):
        drain(r2.at[mb, k], s_at("s2" + tag, mb, k, "r"))
        rr = at(x * tk, tk)
        res = own[mb, k, rr, :] + r1[mb, k, rr, :].astype(F32)
        for dx in range(NX - 1):
            res = res + r2[mb, k, dx].astype(F32)
        return res

    def activate(mb, k):
        gu = total("gu", owngu, r1gu, r2gu, mb, k)
        dn = total("d", ownd, r1d, r2d, mb, k)
        p = prob[mb, k * tk : (k + 1) * tk, :]
        p = jnp.concatenate([p] * (hid // 128), axis=1)
        gate, up = gu[:, :hid], gu[:, hid:]
        down = p * dn
        sig = jax.nn.sigmoid(gate)
        silu = gate * sig
        mine = at(block * tk, tk)
        act[mb, k, mine, 0:hid] = (down * up * sig * (1.0 + gate * (1.0 - sig))).astype(BF)
        act[mb, k, mine, hid : 2 * hid] = (down * silu).astype(BF)
        act[mb, k, mine, 2 * hid : 3 * hid] = (p * (silu * up)).astype(BF)
        ss, rs = s_at("ag", mb, k, "s"), s_at("ag", mb, k, "r")
        piece = act.at[mb, k, mine]
        for dx in (2, 1, 3):
            rdma(piece, piece, ss, rs, member(dx, 0)[2])
        sends.append((ss, act.at[mb, k, pl.ds(0, 3 * tk)]))

    def forward(mb, k):
        drain(act.at[mb, k, pl.ds(0, 3 * tk)], s_at("ag", mb, k, "r"))
        ss = s_at("fw", mb, k, "s")
        piece = act.at[mb, k, at(c * four, four)]
        rdma(piece, piece, ss, s_at("fw", mb, k, "r"), core_peer)
        sends.append((ss, act.at[mb, k, pl.ds(0, four)]))

    def spread_acts(mb, k):
        drain(act.at[mb, k, pl.ds(0, four)], s_at("fw", mb, k, "r"))

        def one(i, carry):
            r = at(i * tile, tile)
            second = wide_mask(mb, k, i * tile, tile)
            first = 1.0 - second
            for j in range(3):
                a = act[mb, k, r, j * hid : (j + 1) * hid].astype(F32)
                lo, hi = (a * first).astype(BF), (a * second).astype(BF)
                if j < 2:
                    amask[mb, k, r, 2 * j * hid : (2 * j + 1) * hid] = lo
                    amask[mb, k, r, (2 * j + 1) * hid : (2 * j + 2) * hid] = hi
                else:
                    shm[mb, k, r, 0:hid] = lo
                    shm[mb, k, r, hid : 2 * hid] = hi
            return carry

        lax.fori_loop(0, rows // tile, one, 0)

    def new_grad(mb, k, r, size):
        rr = at(r, size)
        res = dot_t(amask[mb, k, rr, :], wgu[...])
        return (gs[mb, k, rr, :].astype(F32) + res).astype(BF)

    def relay(k):
        @pl.when(sec > 0)
        def _():
            def one(i, carry):
                r = at(i * tile, tile)
                sent[k, r, :] = new_grad(0, k, i * tile, tile)
                rdma(sent.at[k, r], gs.at[1, k, r], s_at("shift", k, "s"), s_at("g", 1, k, "r"), before)
                return carry

            lax.fori_loop(0, rows // tile, one, 0)

    def give_back(k):
        ss, rs = s_at("back", k, "s"), s_at("back", k, "r")
        for dx, dc in [(2, 0), (2, 1), (1, 0), (1, 1), (3, 0), (3, 1), (0, 1), (0, 0)]:
            px, pc, device = member(dx, dc)
            pos = (pc * NX + px) * tk
            bk[k, at(pos, tk), :] = new_grad(1, k, pos, tk)
            for h in range(2):
                a = bk.at[k, at(pos, tk), pl.ds(h * half, half)]
                b = back_ref.at[0, pl.ds(k * tk, tk), pl.ds(cols_of(x, c, h), half)]
                if (dx, dc) == (0, 0):
                    pltpu.make_async_copy(a, b, rs).start()
                else:
                    rdma(a, b, ss, rs, device)
        sends.append((ss, bk.at[k, pl.ds(0, rows - tk)]))

    def turn_x(mb, k):
        for i in range(wide // 256):
            xt[i * 256 : (i + 1) * 256, :] = jnp.transpose(xs[mb, k, :, i * 256 : (i + 1) * 256])

    def turn_s(mb, k):
        for i in range(2 * hid // 256):
            sht[i * 256 : (i + 1) * 256, :] = jnp.transpose(shm[mb, k, :, i * 256 : (i + 1) * 256])

    def grads(mb, k, first, last):
        turn_x(mb, k)
        turn_s(mb, k)
        for h in (1, 0):
            hs = slice(h * half, (h + 1) * half)
            for j in range(4):
                cs = slice(j * hid, (j + 1) * hid)
                res = dot(xt[hs, :], amask[mb, k, :, cs])
                if not first:
                    res = res + accgu[hs, cs]
                if last and h == 1:
                    pgu[j] = (res * scale).astype(BF)
                    ss = s_at("pgu", j, "s")
                    rdma(pgu.at[j], qgu.at[j], ss, s_at("pgu", j, "r"), y_peer)
                    sends.append((ss, pgu.at[j]))
                else:
                    accgu[hs, cs] = res
            for e in range(2):
                es = slice(e * hid, (e + 1) * hid)
                res = dot(sht[es, :], gs[mb, k, :, hs])
                if not first:
                    res = res + accd[es, hs]
                if last and h == 1:
                    pd[e] = (res * scale).astype(BF)
                    ss = s_at("pd", e, "s")
                    rdma(pd.at[e], qd.at[e], ss, s_at("pd", e, "r"), y_peer)
                    sends.append((ss, pd.at[e]))
                else:
                    accd[es, hs] = res

    def finish():
        for j, (ref, e) in enumerate([(dg_ref, 0), (dg_ref, 1), (du_ref, 0), (du_ref, 1)]):
            drain(qgu.at[j], s_at("pgu", j, "r"))
            ref[0, e] = accgu[0:half, j * hid : (j + 1) * hid] * scale + qgu[j].astype(F32)
        for e in range(2):
            drain(qd.at[e], s_at("pd", e, "r"))
            dd_ref[0, e] = accd[e * hid : (e + 1) * hid, 0:half] * scale + qd[e].astype(F32)

    spread_meta()
    weights()
    for k in range(n_ch):
        spread_x(0, k)
        spread_g(k)
    masks()
    drain(wgu, s_at("wgu", "r"))
    drain(wdn, s_at("wd", "r"))
    for k in range(n_ch):
        wait_x(0, k)
        pre_gu(0, k)
        wait_g(0, k)
        pre_d(0, k)
        mid_gu(0, k)
        mid_d(0, k)
        if k > 0:
            activate(0, k - 1)
    activate(0, n_ch - 1)
    for k in range(n_ch):
        spread_x(1, k)
        spread_last(k)
    for k in range(n_ch):
        forward(0, k)
        spread_acts(0, k)
        relay(k)
    for k in range(n_ch):
        grads(0, k, k == 0, False)
    for k in range(n_ch):
        wait_x(1, k)
        pre_gu(1, k)
        mid_gu(1, k)
    for k in range(n_ch):
        wait_g(1, k)
        pre_d(1, k)
        mid_d(1, k)
        activate(1, k)
        forward(1, k)
        spread_acts(1, k)
        if k < n_ch - 1:
            give_back(k)
        grads(1, k, False, k == n_ch - 1)
        if k == n_ch - 1:
            give_back(k)
    finish()
    for k in range(n_ch):
        @pl.when(sec > 0)
        def _():
            drain(sent.at[k], s_at("shift", k, "s"))

        @pl.when(sec == n_sec - 1)
        def _():
            drain(gs.at[1, k, pl.ds(0, rows - tk)], s_at("last", k, "s"))
        drain(bk.at[k], s_at("back", k, "r"))
    for s, ref in sends:
        drain(ref, s)
    assert names.count <= n_sems, names.count


def body(tokens_in, grad_first, grad_last, expert_ids, gate_probs, w_gate, w_up, w_down):
    tok, width = tokens_in.shape[2:]
    half, hid = w_gate.shape[2:]
    wide = 2 * half
    tk = tok // CHUNKS
    rows, four = 2 * NX * tk, NX * tk
    meta = jnp.concatenate(
        [expert_ids[0, :, :, 0].astype(F32), gate_probs[0], jnp.zeros((4, tok), F32)], axis=0
    )
    n_sems = 40 + 44 * CHUNKS
    pair = (2, CHUNKS)
    scratch = [
        pltpu.VMEM(pair + (rows, wide), BF),
        pltpu.VMEM(pair + (rows, wide), BF),
        pltpu.VMEM((CHUNKS, rows, wide), BF),
        pltpu.VMEM((CHUNKS, rows, wide), BF),
        pltpu.VMEM((wide, 4 * hid), BF),
        pltpu.VMEM((2 * hid, wide), BF),
        pltpu.VMEM((2 * NX, 8, tok), F32),
        pltpu.VMEM(pair + (rows, 128), F32),
        pltpu.VMEM((2, tok, 128), F32),
        pltpu.VMEM((wide, rows), BF),
        pltpu.VMEM((2 * hid, rows), BF),
        pltpu.VMEM(pair + (rows, 3 * hid), BF),
        pltpu.VMEM(pair + (rows, 4 * hid), BF),
        pltpu.VMEM(pair + (rows, 2 * hid), BF),
    ]
    for cols in (2 * hid, hid):
        scratch += [
            pltpu.VMEM(pair + (four, cols), BF),
            pltpu.VMEM(pair + (four, cols), BF),
            pltpu.VMEM(pair + (four, cols), F32),
            pltpu.VMEM(pair + (NX - 1, tk, cols), BF),
            pltpu.VMEM(pair + (NX - 1, tk, cols), BF),
        ]
    scratch += [
        pltpu.VMEM((wide, 4 * hid), F32),
        pltpu.VMEM((2 * hid, wide), F32),
        pltpu.VMEM((4, half, hid), BF),
        pltpu.VMEM((2, hid, half), BF),
        pltpu.VMEM((4, half, hid), BF),
        pltpu.VMEM((2, hid, half), BF),
        pltpu.SemaphoreType.DMA((n_sems,)),
    ]
    vmem = pl.BlockSpec(memory_space=pltpu.VMEM)
    hbm = pl.BlockSpec(memory_space=pl.ANY)
    return pl.pallas_call(
        functools.partial(kernel, (wide, half, hid), tok, n_sems),
        out_shape=(
            jax.ShapeDtypeStruct((1, tok, width), BF),
            jax.ShapeDtypeStruct(w_gate.shape, F32),
            jax.ShapeDtypeStruct(w_up.shape, F32),
            jax.ShapeDtypeStruct(w_down.shape, F32),
        ),
        in_specs=[hbm, hbm, hbm, vmem, hbm, hbm, hbm],
        out_specs=(vmem,) * 4,
        scratch_shapes=scratch,
        compiler_params=pltpu.CompilerParams(
            collective_id=0, has_side_effects=True, vmem_limit_bytes=60 << 20
        ),
        name="section",
    )(tokens_in, grad_first, grad_last, meta, w_gate, w_up, w_down)


def solution(mesh):
    placed = (
        P("pipe", None, "dp", None),
        P("pipe", "dp", None),
        P("dp", None),
        P("pipe", None, "dp", None),
        P("pipe", None, "dp"),
        P("pipe", None, "dp", None),
        P("pipe", None, "dp", None),
        P("pipe", None, None, "dp"),
    )
    return jax.shard_map(
        body,
        mesh=mesh,
        in_specs=placed,
        out_specs=(
            P("pipe", "dp", None),
            P("pipe", None, "dp", None),
            P("pipe", None, "dp", None),
            P("pipe", None, None, "dp"),
        ),
        check_vma=False,
    )
```

```python
import functools
import math

import jax
import jax.numpy as jnp
from jax import lax
from jax.experimental import pallas as pl
from jax.experimental.pallas import tpu as pltpu
from jax.sharding import PartitionSpec as P

MESH = pl.DeviceIdType.MESH
BF = jnp.bfloat16
F32 = jnp.float32

NX = 4
CHUNKS = 2


def dot(a, b):
    return lax.dot_general(a, b, (((1,), (0,)), ((), ())), preferred_element_type=F32)


def dot_t(a, b):
    return lax.dot_general(a, b, (((1,), (1,)), ((), ())), preferred_element_type=F32)


class Sems:
    def __init__(self):
        self.count = 0
        self.index = {}

    def __call__(self, *key):
        if key not in self.index:
            self.index[key] = self.count
            self.count += 1
        return self.index[key]


ORDER = [
    ("spread_meta",), ("weights_gu",), ("spread_x", 0, 0), ("spread_g", 0), ("weights_d",), ("masks",),
    ("wait_x", 0, 0), ("spread_x", 0, 1), ("spread_last",),
    ("wait_gu",), ("pre_gu", 0, 0), ("mid_gu", 0, 0), ("turn_x", 0, 0), ("wait_g", 0, 0), ("wait_d",), ("pre_d", 0, 0), ("mid_d", 0, 0),
    ("wait_x", 0, 1), ("pre_gu", 0, 1), ("activate", 0, 0), ("spread_g", 1), ("mid_gu", 0, 1), ("relay_last",),
    ("forward", 0, 0), ("spread_acts", 0, 0), ("relay", 0),
    ("turn_x", 0, 1), ("wait_g", 0, 1), ("pre_d", 0, 1), ("mid_d", 0, 1), ("activate", 0, 1), ("spread_x", 1, 0),
    ("forward", 0, 1), ("spread_x", 1, 1), ("spread_acts", 0, 1), ("relay", 1), ("grads", 0, 0), ("grads", 0, 1),
    ("wait_x", 1, 0), ("pre_gu", 1, 0), ("mid_gu", 1, 0), ("turn_x", 1, 0), ("wait_g", 1, 0), ("pre_d", 1, 0), ("mid_d", 1, 0),
    ("wait_x", 1, 1), ("pre_gu", 1, 1), ("mid_gu", 1, 1), ("activate", 1, 0), ("turn_x", 1, 1),
    ("wait_g", 1, 1), ("pre_d", 1, 1), ("forward", 1, 0), ("mid_d", 1, 1), ("spread_acts", 1, 0),
    ("activate", 1, 1), ("grads", 1, 0), ("forward", 1, 1), ("spread_acts", 1, 1), ("grads", 1, 1), ("give_back", 0), ("give_back", 1), ("finish",),
]


def schedule(n):
    return ORDER


def kernel(
    dims, tok, n_sems,
    x_ref, g1_ref, gl_ref, ids_ref, p_ref, wg_ref, wu_ref, wd_ref,
    back_ref, dg_ref, du_ref, dd_ref,
    xs, gs, glq, sent, bk, wgu, wdn, metas, msk, prob, xt, sht, act, amask, shm,
    p1gu, r1gu, owngu, s2gu, r2gu, p1d, r1d, ownd, s2d, r2d,
    accgu, accd, pgu, pd, qgu, qd, sem,
):
    wide, half, hid = dims
    n_ch = CHUNKS
    tk = tok // n_ch
    rows = 2 * NX * tk
    four = NX * tk
    tile = min(256, four)
    scale = 1.0 / math.sqrt(tok * lax.axis_size("dp"))

    dp = lax.axis_index("dp")
    sec = lax.axis_index("pipe")
    n_sec = lax.axis_size("pipe")
    x = lax.div(dp, 4)
    yh = lax.rem(lax.div(dp, 2), 2)
    c = lax.rem(dp, 2)
    oc = 1 - c
    block = c * NX + x

    def member(dx, dc):
        px = lax.rem(x + dx, NX)
        pc = lax.rem(c + dc, 2)
        return px, pc, (px * 4 + yh * 2 + pc, sec)

    core_peer = (x * 4 + yh * 2 + oc, sec)
    y_peer = (x * 4 + (1 - yh) * 2 + c, sec)
    before = (dp, lax.rem(sec + n_sec - 1, n_sec))
    after = (dp, lax.rem(sec + 1, n_sec))
    offsets = [(1, 0), (3, 0), (1, 1), (3, 1), (2, 0), (2, 1), (0, 1)]

    names = Sems()
    sends = []

    def s_at(*key):
        return sem.at[names(*key)]

    def rdma(src, dst, ssem, rsem, device):
        pltpu.make_async_remote_copy(
            src_ref=src, dst_ref=dst, send_sem=ssem, recv_sem=rsem,
            device_id=device, device_id_type=MESH,
        ).start()

    def drain(ref, s):
        pltpu.make_async_copy(ref, ref, s).wait()

    def cols_of(px, pc, h):
        return pl.multiple_of(half * (px * 4 + lax.rem(yh + h, 2) * 2 + pc), 128)

    def at(start, size):
        return pl.ds(pl.multiple_of(start, 16), size)

    bar = pltpu.get_barrier_semaphore()
    for dx, dc in offsets:
        pl.semaphore_signal(bar, inc=1, device_id=member(dx, dc)[2], device_id_type=MESH)
    pl.semaphore_signal(bar, inc=1, device_id=y_peer, device_id_type=MESH)
    pl.semaphore_signal(bar, inc=1, device_id=after, device_id_type=MESH)

    @pl.when(sec == n_sec - 1)
    def _():
        for q in range(3):
            pl.semaphore_signal(bar, inc=1, device_id=(dp, 2 * q + 1), device_id_type=MESH)

    helper = jnp.where((lax.rem(sec, 2) == 1) & (sec < n_sec - 1), 1, 0)
    pl.semaphore_wait(bar, len(offsets) + 2 + helper)

    def spread_meta():
        ss, rs = s_at("meta", "s"), s_at("meta", "r")
        for dx, dc in offsets:
            rdma(ids_ref, metas.at[block], ss, rs, member(dx, dc)[2])
        pltpu.make_async_copy(ids_ref, metas.at[block], rs).start()
        sends.append((ss, metas.at[pl.ds(0, len(offsets))]))

    def masks():
        drain(metas, s_at("meta", "r"))
        for mb in range(2):
            for b in range(2 * NX):
                row = metas[b, mb : mb + 1, :].astype(F32)
                col = jnp.transpose(jnp.broadcast_to(row, (128, 128)))
                for k in range(n_ch):
                    msk[mb, k, b * tk : (b + 1) * tk, :] = col[k * tk : (k + 1) * tk, :]
            row = p_ref[mb : mb + 1, :]
            prob[mb] = jnp.transpose(jnp.broadcast_to(row, (128, 128)))

    def weights_gu():
        ss, rs = s_at("wgu", "s"), s_at("wgu", "r")
        for j, (ref, e) in enumerate([(wg_ref, 0), (wg_ref, 1), (wu_ref, 0), (wu_ref, 1)]):
            src = ref.at[0, e]
            cs = pl.ds(j * hid, hid)
            rdma(src, wgu.at[pl.ds(half, half), cs], ss, rs, y_peer)
            pltpu.make_async_copy(src, wgu.at[pl.ds(0, half), cs], rs).start()
        sends.append((ss, wgu.at[pl.ds(0, half)]))

    def weights_d():
        ss, rs = s_at("wd", "s"), s_at("wd", "r")
        for e in range(2):
            src = wd_ref.at[0, e]
            rr = pl.ds(e * hid, hid)
            rdma(src, wdn.at[rr, pl.ds(half, half)], ss, rs, y_peer)
            pltpu.make_async_copy(src, wdn.at[rr, pl.ds(0, half)], rs).start()
        sends.append((ss, wdn.at[:, pl.ds(0, half)]))

    def wait_gu():
        drain(wgu, s_at("wgu", "r"))

    def wait_d():
        drain(wdn, s_at("wd", "r"))

    def spread(src, dst, start, size, place, ss, rs):
        for dx, dc in offsets + [(0, 0)]:
            px, pc, device = member(dx, dc)
            for h in range(2):
                a = src.at[pl.ds(start, size), pl.ds(cols_of(px, pc, h), half)]
                b = dst.at[at(place, size), pl.ds(h * half, half)]
                if (dx, dc) == (0, 0):
                    pltpu.make_async_copy(a, b, rs).start()
                else:
                    rdma(a, b, ss, rs, device)

    def spread_x(mb, k):
        ss = s_at("x", "s")
        spread(x_ref.at[0, mb], xs.at[mb, k], k * tk, tk, block * tk, ss, s_at("x", mb, k, "r"))

    def spread_g(k):
        ss = s_at("g", "s")
        spread(g1_ref.at[0], gs.at[0, k], k * tk, tk, block * tk, ss, s_at("g", 0, k, "r"))

    def quarter(q):
        per = 4 // n_ch
        size = tk // per
        return q // per, (q % per) * size, size

    def spread_last():
        for q in range(4):
            @pl.when(sec == 2 * q + 1)
            def _():
                k, base, size = quarter(q)
                if q < 3:
                    rs = s_at("lastq", "r")
                    spread(gl_ref, glq, k * tk + base, size, block * size, s_at("last", "s"), rs)
                else:
                    rs = s_at("g", 1, k, "r")
                    spread(gl_ref, gs.at[1, k], k * tk + base, size, block * tk + base, s_at("last", "s"), rs)

    def relay_last():
        for q in range(3):
            @pl.when(sec == 2 * q + 1)
            def _():
                k, base, size = quarter(q)
                drain(glq, s_at("lastq", "r"))
                for b in range(2 * NX):
                    rdma(
                        glq.at[pl.ds(b * size, size)], gs.at[1, k, pl.ds(b * tk + base, size)],
                        s_at("lastq", "s"), s_at("g", 1, k, "r"), (dp, n_sec - 1),
                    )

    def wait_x(mb, k):
        drain(xs.at[mb, k], s_at("x", mb, k, "r"))

    def wait_g(mb, k):
        drain(gs.at[mb, k], s_at("g", mb, k, "r"))

    def wide_mask(mb, k, start, size):
        m = msk[mb, k, at(start, size), :]
        return jnp.concatenate([m] * (hid // 128), axis=1)

    def pre_gu(mb, k):
        def step(base, out, out_base, kind):
            def one(i, carry):
                r = base + i * tile
                lhs = xs[mb, k, at(r, tile), :]
                second = wide_mask(mb, k, r, tile) != 0.0
                for part in range(2):
                    res = dot(lhs, wgu[:, part * 2 * hid : (part + 1) * 2 * hid])
                    pick = jnp.where(second, res[:, hid:], res[:, :hid])
                    out[mb, k, at(out_base + i * tile, tile), part * hid : (part + 1) * hid] = pick.astype(kind)
                return carry

            lax.fori_loop(0, four // tile, one, 0)

        step(oc * four, p1gu, 0, BF)
        ss = s_at("p1gu", "s")
        rdma(p1gu.at[mb, k], r1gu.at[mb, k], ss, s_at("p1gu", mb, k, "r"), core_peer)
        step(c * four, owngu, 0, F32)

    def pre_d(mb, k):
        def step(base, out, kind):
            def one(i, carry):
                r = base + i * tile
                res = dot_t(gs[mb, k, at(r, tile), :], wdn[...])
                second = wide_mask(mb, k, r, tile) != 0.0
                pick = jnp.where(second, res[:, hid:], res[:, :hid])
                out[mb, k, at(i * tile, tile), :] = pick.astype(kind)
                return carry

            lax.fori_loop(0, four // tile, one, 0)

        step(oc * four, p1d, BF)
        ss = s_at("p1d", "s")
        rdma(p1d.at[mb, k], r1d.at[mb, k], ss, s_at("p1d", mb, k, "r"), core_peer)
        step(c * four, ownd, F32)

    def along_x(tag, own, r1, s2, r2, mb, k):
        drain(r1.at[mb, k], s_at("p1" + tag, mb, k, "r"))
        ss, rs = s_at("s2" + tag, "s"), s_at("s2" + tag, mb, k, "r")
        for dx in (2, 1, 3):
            px, _, device = member(dx, 0)
            rr = at(px * tk, tk)
            s2[mb, k, dx - 1] = (own[mb, k, rr, :] + r1[mb, k, rr, :].astype(F32)).astype(BF)
            rdma(s2.at[mb, k, dx - 1], r2.at[mb, k, dx - 1], ss, rs, device)

    def mid_gu(mb, k):
        along_x("gu", owngu, r1gu, s2gu, r2gu, mb, k)

    def mid_d(mb, k):
        along_x("d", ownd, r1d, s2d, r2d, mb, k)

    def total(tag, own, r1, r2, mb, k):
        drain(r2.at[mb, k], s_at("s2" + tag, mb, k, "r"))
        rr = at(x * tk, tk)
        res = own[mb, k, rr, :] + r1[mb, k, rr, :].astype(F32)
        for dx in range(NX - 1):
            res = res + r2[mb, k, dx].astype(F32)
        return res

    def activate(mb, k):
        gu = total("gu", owngu, r1gu, r2gu, mb, k)
        dn = total("d", ownd, r1d, r2d, mb, k)
        p = prob[mb, k * tk : (k + 1) * tk, :]
        p = jnp.concatenate([p] * (hid // 128), axis=1)
        gate, up = gu[:, :hid], gu[:, hid:]
        down = p * dn
        sig = jax.nn.sigmoid(gate)
        silu = gate * sig
        mine = at(block * tk, tk)
        act[mb, k, mine, 0:hid] = (down * up * sig * (1.0 + gate * (1.0 - sig))).astype(BF)
        act[mb, k, mine, hid : 2 * hid] = (down * silu).astype(BF)
        act[mb, k, mine, 2 * hid : 3 * hid] = (p * (silu * up)).astype(BF)
        ss, rs = s_at("ag", "s"), s_at("ag", mb, k, "r")
        piece = act.at[mb, k, mine]
        for dx in (2, 1, 3):
            rdma(piece, piece, ss, rs, member(dx, 0)[2])

    def forward(mb, k):
        drain(act.at[mb, k, pl.ds(0, 3 * tk)], s_at("ag", mb, k, "r"))
        ss = s_at("fw", "s")
        piece = act.at[mb, k, at(c * four, four)]
        rdma(piece, piece, ss, s_at("fw", mb, k, "r"), core_peer)

    def spread_acts(mb, k):
        drain(act.at[mb, k, pl.ds(0, four)], s_at("fw", mb, k, "r"))

        def one(i, carry):
            r = at(i * tile, tile)
            second = wide_mask(mb, k, i * tile, tile)
            first = 1.0 - second
            for j in range(3):
                a = act[mb, k, r, j * hid : (j + 1) * hid].astype(F32)
                lo, hi = (a * first).astype(BF), (a * second).astype(BF)
                if j < 2:
                    amask[mb, k, r, 2 * j * hid : (2 * j + 1) * hid] = lo
                    amask[mb, k, r, (2 * j + 1) * hid : (2 * j + 2) * hid] = hi
                else:
                    shm[mb, k, r, 0:hid] = lo
                    shm[mb, k, r, hid : 2 * hid] = hi
            return carry

        lax.fori_loop(0, rows // tile, one, 0)

    def new_grad(mb, k, r, size):
        rr = at(r, size)
        res = dot_t(amask[mb, k, rr, :], wgu[...])
        return (gs[mb, k, rr, :].astype(F32) + res).astype(BF)

    def relay(k):
        @pl.when(sec > 0)
        def _():
            def one(i, carry):
                r = at(i * tile, tile)
                sent[k, r, :] = new_grad(0, k, i * tile, tile)
                rdma(sent.at[k, r], gs.at[1, k, r], s_at("shift", "s"), s_at("g", 1, k, "r"), before)
                return carry

            lax.fori_loop(0, rows // tile, one, 0)

    def give_back(k):
        ss, rs = s_at("back", "s"), s_at("back", "r")
        for dx, dc in [(2, 0), (2, 1), (1, 0), (1, 1), (3, 0), (3, 1), (0, 1), (0, 0)]:
            px, pc, device = member(dx, dc)
            pos = (pc * NX + px) * tk
            bk[k, at(pos, tk), :] = new_grad(1, k, pos, tk)
            for h in range(2):
                a = bk.at[k, at(pos, tk), pl.ds(h * half, half)]
                b = back_ref.at[0, pl.ds(k * tk, tk), pl.ds(cols_of(x, c, h), half)]
                if (dx, dc) == (0, 0):
                    pltpu.make_async_copy(a, b, rs).start()
                else:
                    rdma(a, b, ss, rs, device)

    def turn_x(mb, k):
        for i in range(wide // 256):
            xt[mb, k, i * 256 : (i + 1) * 256, :] = jnp.transpose(xs[mb, k, :, i * 256 : (i + 1) * 256])

    def turn_s(mb, k):
        for i in range(2 * hid // 256):
            sht[i * 256 : (i + 1) * 256, :] = jnp.transpose(shm[mb, k, :, i * 256 : (i + 1) * 256])

    def grads(mb, k):
        first, last = (mb, k) == (0, 0), (mb, k) == (1, n_ch - 1)
        turn_s(mb, k)
        for h in (1, 0):
            hs = slice(h * half, (h + 1) * half)
            for j in range(4):
                cs = slice(j * hid, (j + 1) * hid)
                res = dot(xt[mb, k, hs, :], amask[mb, k, :, cs])
                if not first:
                    res = res + accgu[hs, cs]
                if last and h == 1:
                    pgu[j] = (res * scale).astype(BF)
                    ss = s_at("pgu", "s")
                    rdma(pgu.at[j], qgu.at[j], ss, s_at("pgu", j, "r"), y_peer)
                else:
                    accgu[hs, cs] = res
            for e in range(2):
                es = slice(e * hid, (e + 1) * hid)
                res = dot(sht[es, :], gs[mb, k, :, hs])
                if not first:
                    res = res + accd[es, hs]
                if last and h == 1:
                    pd[e] = (res * scale).astype(BF)
                    ss = s_at("pd", "s")
                    rdma(pd.at[e], qd.at[e], ss, s_at("pd", e, "r"), y_peer)
                else:
                    accd[es, hs] = res

    def finish():
        for j, (ref, e) in enumerate([(dg_ref, 0), (dg_ref, 1), (du_ref, 0), (du_ref, 1)]):
            drain(qgu.at[j], s_at("pgu", j, "r"))
            ref[0, e] = accgu[0:half, j * hid : (j + 1) * hid] * scale + qgu[j].astype(F32)
        for e in range(2):
            drain(qd.at[e], s_at("pd", e, "r"))
            dd_ref[0, e] = accd[e * hid : (e + 1) * hid, 0:half] * scale + qd[e].astype(F32)

    steps = dict(
        spread_meta=spread_meta, weights_gu=weights_gu, weights_d=weights_d, masks=masks,
        wait_gu=wait_gu, wait_d=wait_d, turn_x=turn_x,
        spread_x=spread_x, spread_g=spread_g, spread_last=spread_last, relay_last=relay_last,
        wait_x=wait_x, wait_g=wait_g, pre_gu=pre_gu, pre_d=pre_d, mid_gu=mid_gu, mid_d=mid_d,
        activate=activate, forward=forward, spread_acts=spread_acts, relay=relay,
        give_back=give_back, grads=grads, finish=finish,
    )
    for name, *where in schedule(n_ch):
        steps[name](*where)
    @pl.when(sec > 0)
    def _():
        drain(sent, s_at("shift", "s"))

    drain(bk, s_at("back", "r"))
    for tag, ref in (
        ("x", xs.at[:, :, pl.ds(0, rows - tk)]), ("g", gs.at[0, :, pl.ds(0, rows - tk)]),
        ("p1gu", p1gu), ("p1d", p1d), ("s2gu", s2gu), ("s2d", s2d),
        ("ag", act.at[:, :, pl.ds(0, 3 * tk)]), ("fw", act.at[:, :, pl.ds(0, four)]),
        ("back", bk.at[:, pl.ds(0, rows - tk)]), ("pgu", pgu), ("pd", pd),
    ):
        drain(ref, s_at(tag, "s"))

    @pl.when(lax.rem(sec, 2) == 1)
    def _():
        drain(glq.at[pl.ds(0, rows // 4 * n_ch - tok // 4)], s_at("last", "s"))

    @pl.when((lax.rem(sec, 2) == 1) & (sec < n_sec - 1))
    def _():
        drain(glq, s_at("lastq", "s"))

    for s, ref in sends:
        drain(ref, s)
    assert names.count == n_sems, names.count


def write_out(*refs):
    sem = refs[-1]
    copies = []
    for i in range(4):
        rows = refs[i].shape[-2] // 4
        for j in range(4):
            part = (Ellipsis, pl.ds(j * rows, rows), slice(None))
            copies.append(pltpu.make_async_copy(refs[i].at[part], refs[4 + i].at[part], sem.at[4 * i + j]))
    for copy in copies:
        copy.start()
    for copy in copies:
        copy.wait()


def body(tokens_in, grad_first, grad_last, expert_ids, gate_probs, w_gate, w_up, w_down):
    tok, width = tokens_in.shape[2:]
    half, hid = w_gate.shape[2:]
    wide = 2 * half
    tk = tok // CHUNKS
    rows, four = 2 * NX * tk, NX * tk
    n_sems = 20 + 20 * CHUNKS
    pair = (2, CHUNKS)
    scratch = [
        pltpu.VMEM(pair + (rows, wide), BF),
        pltpu.VMEM(pair + (rows, wide), BF),
        pltpu.VMEM((2 * NX * tok // 4, wide), BF),
        pltpu.VMEM((CHUNKS, rows, wide), BF),
        pltpu.VMEM((CHUNKS, rows, wide), BF),
        pltpu.VMEM((wide, 4 * hid), BF),
        pltpu.VMEM((2 * hid, wide), BF),
        pltpu.VMEM((2 * NX, 2, tok), jnp.int32),
        pltpu.VMEM(pair + (rows, 128), F32),
        pltpu.VMEM((2, tok, 128), F32),
        pltpu.VMEM(pair + (wide, rows), BF),
        pltpu.VMEM((2 * hid, rows), BF),
        pltpu.VMEM(pair + (rows, 3 * hid), BF),
        pltpu.VMEM(pair + (rows, 4 * hid), BF),
        pltpu.VMEM(pair + (rows, 2 * hid), BF),
    ]
    for cols in (2 * hid, hid):
        scratch += [
            pltpu.VMEM(pair + (four, cols), BF),
            pltpu.VMEM(pair + (four, cols), BF),
            pltpu.VMEM(pair + (four, cols), F32),
            pltpu.VMEM(pair + (NX - 1, tk, cols), BF),
            pltpu.VMEM(pair + (NX - 1, tk, cols), BF),
        ]
    scratch += [
        pltpu.VMEM((wide, 4 * hid), F32),
        pltpu.VMEM((2 * hid, wide), F32),
        pltpu.VMEM((4, half, hid), BF),
        pltpu.VMEM((2, hid, half), BF),
        pltpu.VMEM((4, half, hid), BF),
        pltpu.VMEM((2, hid, half), BF),
        pltpu.SemaphoreType.DMA((n_sems,)),
    ]
    vmem = pl.BlockSpec(memory_space=pltpu.VMEM)
    hbm = pl.BlockSpec(memory_space=pl.ANY)
    results = pl.pallas_call(
        functools.partial(kernel, (wide, half, hid), tok, n_sems),
        out_shape=(
            jax.ShapeDtypeStruct((1, tok, width), BF),
            jax.ShapeDtypeStruct(w_gate.shape, F32),
            jax.ShapeDtypeStruct(w_up.shape, F32),
            jax.ShapeDtypeStruct(w_down.shape, F32),
        ),
        in_specs=[hbm, hbm, hbm, vmem, vmem, hbm, hbm, hbm],
        out_specs=(vmem,) * 4,
        scratch_shapes=scratch,
        compiler_params=pltpu.CompilerParams(
            collective_id=0, has_side_effects=True, vmem_limit_bytes=60 << 20
        ),
        name="section",
    )(
        tokens_in, grad_first, grad_last, expert_ids.reshape(2, tok), gate_probs.reshape(2, tok),
        w_gate, w_up, w_down,
    )
    return pl.pallas_call(
        write_out,
        out_shape=tuple(jax.ShapeDtypeStruct(r.shape, r.dtype) for r in results),
        in_specs=[vmem] * 4,
        out_specs=(hbm,) * 4,
        scratch_shapes=[pltpu.SemaphoreType.DMA((16,))],
        name="write_out",
    )(*results)


def solution(mesh):
    placed = (
        P("pipe", None, "dp", None),
        P("pipe", "dp", None),
        P("dp", None),
        P("pipe", None, "dp", None),
        P("pipe", None, "dp"),
        P("pipe", None, "dp", None),
        P("pipe", None, "dp", None),
        P("pipe", None, None, "dp"),
    )
    return jax.shard_map(
        body,
        mesh=mesh,
        in_specs=placed,
        out_specs=(
            P("pipe", "dp", None),
            P("pipe", None, "dp", None),
            P("pipe", None, "dp", None),
            P("pipe", None, None, "dp"),
        ),
        check_vma=False,
    )
```

```python
import functools
import math

import jax
import jax.numpy as jnp
from jax import lax
from jax.experimental import pallas as pl
from jax.experimental.pallas import tpu as pltpu
from jax.sharding import PartitionSpec as P

MESH = pl.DeviceIdType.MESH
BF = jnp.bfloat16
F32 = jnp.float32

NX = 4
CHUNKS = 2


def dot(a, b):
    return lax.dot_general(a, b, (((1,), (0,)), ((), ())), preferred_element_type=F32)


def dot_t(a, b):
    return lax.dot_general(a, b, (((1,), (1,)), ((), ())), preferred_element_type=F32)


class Sems:
    def __init__(self):
        self.count = 0
        self.index = {}

    def __call__(self, *key):
        if key not in self.index:
            self.index[key] = self.count
            self.count += 1
        return self.index[key]


ORDER = [
    ("spread_meta",), ("weights_gu",), ("spread_x", 0, 0), ("spread_g", 0), ("weights_d",), ("masks",),
    ("wait_x", 0, 0), ("spread_x", 0, 1), ("spread_last",),
    ("wait_gu",), ("pre_gu", 0, 0), ("mid_gu", 0, 0), ("turn_x", 0, 0), ("wait_g", 0, 0), ("wait_d",), ("pre_d", 0, 0), ("mid_d", 0, 0),
    ("wait_x", 0, 1), ("pre_gu", 0, 1), ("activate", 0, 0), ("spread_g", 1), ("relay_last",),
    ("forward", 0, 0), ("mid_gu", 0, 1), ("spread_acts", 0, 0), ("relay", 0),
    ("turn_x", 0, 1), ("wait_g", 0, 1), ("pre_d", 0, 1), ("mid_d", 0, 1), ("activate", 0, 1), ("spread_x", 1, 0),
    ("forward", 0, 1), ("spread_acts", 0, 1), ("relay", 1), ("spread_x", 1, 1), ("grads", 0, 0), ("grads", 0, 1),
    ("wait_x", 1, 0), ("pre_gu", 1, 0), ("mid_gu", 1, 0), ("turn_x", 1, 0), ("wait_g", 1, 0), ("pre_d", 1, 0), ("mid_d", 1, 0),
    ("wait_x", 1, 1), ("pre_gu", 1, 1), ("mid_gu", 1, 1), ("activate", 1, 0), ("turn_x", 1, 1),
    ("wait_g", 1, 1), ("pre_d", 1, 1), ("mid_d", 1, 1), ("forward", 1, 0),
    ("activate", 1, 1), ("spread_acts", 1, 0), ("grads", 1, 0), ("forward", 1, 1), ("spread_acts", 1, 1), ("grads", 1, 1), ("give_back", 0), ("give_back", 1), ("finish",),
]


def schedule(n):
    return ORDER


def kernel(
    dims, tok, n_sems,
    x_ref, g1_ref, gl_ref, ids_ref, p_ref, wg_ref, wu_ref, wd_ref,
    back_ref, dg_ref, du_ref, dd_ref,
    xs, gs, glq, sent, bk, wgu, wdn, metas, msk, prob, xt, sht, act, amask, shm,
    p1gu, r1gu, owngu, s2gu, r2gu, p1d, r1d, ownd, s2d, r2d,
    accgu, accd, pgu, pd, qgu, qd, outgu, outd, sem,
):
    wide, half, hid = dims
    n_ch = CHUNKS
    tk = tok // n_ch
    rows = 2 * NX * tk
    four = NX * tk
    tile = min(256, four)
    scale = 1.0 / math.sqrt(tok * lax.axis_size("dp"))

    dp = lax.axis_index("dp")
    sec = lax.axis_index("pipe")
    n_sec = lax.axis_size("pipe")
    x = lax.div(dp, 4)
    yh = lax.rem(lax.div(dp, 2), 2)
    c = lax.rem(dp, 2)
    oc = 1 - c
    block = c * NX + x

    def member(dx, dc):
        px = lax.rem(x + dx, NX)
        pc = lax.rem(c + dc, 2)
        return px, pc, (px * 4 + yh * 2 + pc, sec)

    core_peer = (x * 4 + yh * 2 + oc, sec)
    y_peer = (x * 4 + (1 - yh) * 2 + c, sec)
    before = (dp, lax.rem(sec + n_sec - 1, n_sec))
    after = (dp, lax.rem(sec + 1, n_sec))
    offsets = [(1, 0), (3, 0), (1, 1), (3, 1), (2, 0), (2, 1), (0, 1)]

    names = Sems()
    sends = []

    def s_at(*key):
        return sem.at[names(*key)]

    def rdma(src, dst, ssem, rsem, device):
        pltpu.make_async_remote_copy(
            src_ref=src, dst_ref=dst, send_sem=ssem, recv_sem=rsem,
            device_id=device, device_id_type=MESH,
        ).start()

    def drain(ref, s):
        pltpu.make_async_copy(ref, ref, s).wait()

    def cols_of(px, pc, h):
        return pl.multiple_of(half * (px * 4 + lax.rem(yh + h, 2) * 2 + pc), 128)

    def at(start, size):
        return pl.ds(pl.multiple_of(start, 16), size)

    bar = pltpu.get_barrier_semaphore()
    for dx, dc in offsets:
        pl.semaphore_signal(bar, inc=1, device_id=member(dx, dc)[2], device_id_type=MESH)
    pl.semaphore_signal(bar, inc=1, device_id=y_peer, device_id_type=MESH)
    pl.semaphore_signal(bar, inc=1, device_id=after, device_id_type=MESH)

    @pl.when(sec == n_sec - 1)
    def _():
        for q in range(7):
            pl.semaphore_signal(bar, inc=1, device_id=(dp, q), device_id_type=MESH)

    helper = jnp.where(sec < n_sec - 1, 1, 0)
    pl.semaphore_wait(bar, len(offsets) + 2 + helper)

    def spread_meta():
        ss, rs = s_at("meta", "s"), s_at("meta", "r")
        for dx, dc in offsets:
            rdma(ids_ref, metas.at[block], ss, rs, member(dx, dc)[2])
        pltpu.make_async_copy(ids_ref, metas.at[block], rs).start()
        sends.append((ss, metas.at[pl.ds(0, len(offsets))]))

    def masks():
        drain(metas, s_at("meta", "r"))
        for mb in range(2):
            for b in range(2 * NX):
                row = metas[b, mb : mb + 1, :].astype(F32)
                col = jnp.transpose(jnp.broadcast_to(row, (128, 128)))
                for k in range(n_ch):
                    msk[mb, k, b * tk : (b + 1) * tk, :] = col[k * tk : (k + 1) * tk, :]
            row = p_ref[mb : mb + 1, :]
            prob[mb] = jnp.transpose(jnp.broadcast_to(row, (128, 128)))

    def weights_gu():
        ss, rs = s_at("wgu", "s"), s_at("wgu", "r")
        for j, (ref, e) in enumerate([(wg_ref, 0), (wg_ref, 1), (wu_ref, 0), (wu_ref, 1)]):
            src = ref.at[0, e]
            cs = pl.ds(j * hid, hid)
            rdma(src, wgu.at[pl.ds(half, half), cs], ss, rs, y_peer)
            pltpu.make_async_copy(src, wgu.at[pl.ds(0, half), cs], rs).start()
        sends.append((ss, wgu.at[pl.ds(0, half)]))

    def weights_d():
        ss, rs = s_at("wd", "s"), s_at("wd", "r")
        for e in range(2):
            src = wd_ref.at[0, e]
            rr = pl.ds(e * hid, hid)
            rdma(src, wdn.at[rr, pl.ds(half, half)], ss, rs, y_peer)
            pltpu.make_async_copy(src, wdn.at[rr, pl.ds(0, half)], rs).start()
        sends.append((ss, wdn.at[:, pl.ds(0, half)]))

    def wait_gu():
        drain(wgu, s_at("wgu", "r"))

    def wait_d():
        drain(wdn, s_at("wd", "r"))

    def spread(src, dst, start, size, place, ss, rs):
        for dx, dc in offsets + [(0, 0)]:
            px, pc, device = member(dx, dc)
            for h in range(2):
                a = src.at[pl.ds(start, size), pl.ds(cols_of(px, pc, h), half)]
                b = dst.at[at(place, size), pl.ds(h * half, half)]
                if (dx, dc) == (0, 0):
                    pltpu.make_async_copy(a, b, rs).start()
                else:
                    rdma(a, b, ss, rs, device)

    def spread_x(mb, k):
        ss = s_at("x", "s")
        spread(x_ref.at[0, mb], xs.at[mb, k], k * tk, tk, block * tk, ss, s_at("x", mb, k, "r"))

    def spread_g(k):
        ss = s_at("g", "s")
        spread(g1_ref.at[0], gs.at[0, k], k * tk, tk, block * tk, ss, s_at("g", 0, k, "r"))

    def eighth(q):
        per = 8 // n_ch
        size = tk // per
        return q // per, (q % per) * size, size

    def spread_last():
        for q in range(8):
            @pl.when(sec == q)
            def _():
                k, base, size = eighth(q)
                if q < 7:
                    rs = s_at("lastq", "r")
                    spread(gl_ref, glq, k * tk + base, size, block * size, s_at("last", "s"), rs)
                else:
                    rs = s_at("g", 1, k, "r")
                    spread(gl_ref, gs.at[1, k], k * tk + base, size, block * tk + base, s_at("last", "s"), rs)

    def relay_last():
        for q in range(7):
            @pl.when(sec == q)
            def _():
                k, base, size = eighth(q)
                drain(glq, s_at("lastq", "r"))
                for b in range(2 * NX):
                    rdma(
                        glq.at[pl.ds(b * size, size)], gs.at[1, k, pl.ds(b * tk + base, size)],
                        s_at("lastq", "s"), s_at("g", 1, k, "r"), (dp, n_sec - 1),
                    )

    def wait_x(mb, k):
        drain(xs.at[mb, k], s_at("x", mb, k, "r"))

    def wait_g(mb, k):
        drain(gs.at[mb, k], s_at("g", mb, k, "r"))

    def wide_mask(mb, k, start, size):
        m = msk[mb, k, at(start, size), :]
        return jnp.concatenate([m] * (hid // 128), axis=1)

    def pre_gu(mb, k):
        def step(base, out, out_base, kind):
            def one(i, carry):
                r = base + i * tile
                lhs = xs[mb, k, at(r, tile), :]
                second = wide_mask(mb, k, r, tile) != 0.0
                for part in range(2):
                    res = dot(lhs, wgu[:, part * 2 * hid : (part + 1) * 2 * hid])
                    pick = jnp.where(second, res[:, hid:], res[:, :hid])
                    out[mb, k, at(out_base + i * tile, tile), part * hid : (part + 1) * hid] = pick.astype(kind)
                return carry

            lax.fori_loop(0, four // tile, one, 0)

        step(oc * four, p1gu, 0, BF)
        ss = s_at("p1gu", "s")
        rdma(p1gu.at[mb, k], r1gu.at[mb, k], ss, s_at("p1gu", mb, k, "r"), core_peer)
        step(c * four, owngu, 0, F32)

    def pre_d(mb, k):
        def step(base, out, kind):
            def one(i, carry):
                r = base + i * tile
                res = dot_t(gs[mb, k, at(r, tile), :], wdn[...])
                second = wide_mask(mb, k, r, tile) != 0.0
                pick = jnp.where(second, res[:, hid:], res[:, :hid])
                out[mb, k, at(i * tile, tile), :] = pick.astype(kind)
                return carry

            lax.fori_loop(0, four // tile, one, 0)

        step(oc * four, p1d, BF)
        ss = s_at("p1d", "s")
        rdma(p1d.at[mb, k], r1d.at[mb, k], ss, s_at("p1d", mb, k, "r"), core_peer)
        step(c * four, ownd, F32)

    def along_x(tag, own, r1, s2, r2, mb, k):
        drain(r1.at[mb, k], s_at("p1" + tag, mb, k, "r"))
        ss, rs = s_at("s2" + tag, "s"), s_at("s2" + tag, mb, k, "r")
        for dx in (2, 1, 3):
            px, _, device = member(dx, 0)
            rr = at(px * tk, tk)
            s2[mb, k, dx - 1] = (own[mb, k, rr, :] + r1[mb, k, rr, :].astype(F32)).astype(BF)
            rdma(s2.at[mb, k, dx - 1], r2.at[mb, k, dx - 1], ss, rs, device)

    def mid_gu(mb, k):
        along_x("gu", owngu, r1gu, s2gu, r2gu, mb, k)

    def mid_d(mb, k):
        along_x("d", ownd, r1d, s2d, r2d, mb, k)

    def total(tag, own, r1, r2, mb, k):
        drain(r2.at[mb, k], s_at("s2" + tag, mb, k, "r"))
        rr = at(x * tk, tk)
        res = own[mb, k, rr, :] + r1[mb, k, rr, :].astype(F32)
        for dx in range(NX - 1):
            res = res + r2[mb, k, dx].astype(F32)
        return res

    def activate(mb, k):
        gu = total("gu", owngu, r1gu, r2gu, mb, k)
        dn = total("d", ownd, r1d, r2d, mb, k)
        p = prob[mb, k * tk : (k + 1) * tk, :]
        p = jnp.concatenate([p] * (hid // 128), axis=1)
        gate, up = gu[:, :hid], gu[:, hid:]
        down = p * dn
        sig = jax.nn.sigmoid(gate)
        silu = gate * sig
        mine = at(block * tk, tk)
        act[mb, k, mine, 0:hid] = (down * up * sig * (1.0 + gate * (1.0 - sig))).astype(BF)
        act[mb, k, mine, hid : 2 * hid] = (down * silu).astype(BF)
        act[mb, k, mine, 2 * hid : 3 * hid] = (p * (silu * up)).astype(BF)
        ss, rs = s_at("ag", "s"), s_at("ag", mb, k, "r")
        piece = act.at[mb, k, mine]
        for dx in (2, 1, 3):
            rdma(piece, piece, ss, rs, member(dx, 0)[2])

    def forward(mb, k):
        drain(act.at[mb, k, pl.ds(0, 3 * tk)], s_at("ag", mb, k, "r"))
        ss = s_at("fw", "s")
        piece = act.at[mb, k, at(c * four, four)]
        rdma(piece, piece, ss, s_at("fw", mb, k, "r"), core_peer)

    def spread_acts(mb, k):
        drain(act.at[mb, k, pl.ds(0, four)], s_at("fw", mb, k, "r"))

        def one(i, carry):
            r = at(i * tile, tile)
            second = wide_mask(mb, k, i * tile, tile)
            first = 1.0 - second
            for j in range(3):
                a = act[mb, k, r, j * hid : (j + 1) * hid].astype(F32)
                lo, hi = (a * first).astype(BF), (a * second).astype(BF)
                if j < 2:
                    amask[mb, k, r, 2 * j * hid : (2 * j + 1) * hid] = lo
                    amask[mb, k, r, (2 * j + 1) * hid : (2 * j + 2) * hid] = hi
                else:
                    shm[mb, k, r, 0:hid] = lo
                    shm[mb, k, r, hid : 2 * hid] = hi
            return carry

        lax.fori_loop(0, rows // tile, one, 0)

    def new_grad(mb, k, r, size):
        rr = at(r, size)
        res = dot_t(amask[mb, k, rr, :], wgu[...])
        return (gs[mb, k, rr, :].astype(F32) + res).astype(BF)

    def relay(k):
        @pl.when(sec > 0)
        def _():
            def one(i, carry):
                r = at(i * tile, tile)
                sent[k, r, :] = new_grad(0, k, i * tile, tile)
                rdma(sent.at[k, r], gs.at[1, k, r], s_at("shift", "s"), s_at("g", 1, k, "r"), before)
                return carry

            lax.fori_loop(0, rows // tile, one, 0)

    def give_back(k):
        ss, rs = s_at("back", "s"), s_at("back", "r")
        for dx, dc in [(2, 0), (2, 1), (1, 0), (1, 1), (3, 0), (3, 1), (0, 1), (0, 0)]:
            px, pc, device = member(dx, dc)
            pos = (pc * NX + px) * tk
            bk[k, at(pos, tk), :] = new_grad(1, k, pos, tk)
            for h in range(2):
                a = bk.at[k, at(pos, tk), pl.ds(h * half, half)]
                b = back_ref.at[0, pl.ds(k * tk, tk), pl.ds(cols_of(x, c, h), half)]
                if (dx, dc) == (0, 0):
                    pltpu.make_async_copy(a, b, rs).start()
                else:
                    rdma(a, b, ss, rs, device)

    def turn_x(mb, k):
        for i in range(wide // 256):
            xt[mb, k, i * 256 : (i + 1) * 256, :] = jnp.transpose(xs[mb, k, :, i * 256 : (i + 1) * 256])

    def turn_s(mb, k):
        for i in range(2 * hid // 256):
            sht[i * 256 : (i + 1) * 256, :] = jnp.transpose(shm[mb, k, :, i * 256 : (i + 1) * 256])

    def grads(mb, k):
        first, last = (mb, k) == (0, 0), (mb, k) == (1, n_ch - 1)
        turn_s(mb, k)
        for h in (1, 0):
            hs = slice(h * half, (h + 1) * half)
            for j in range(4):
                cs = slice(j * hid, (j + 1) * hid)
                res = dot(xt[mb, k, hs, :], amask[mb, k, :, cs])
                if not first:
                    res = res + accgu[hs, cs]
                if last and h == 1:
                    pgu[j] = (res * scale).astype(BF)
                    ss = s_at("pgu", "s")
                    rdma(pgu.at[j], qgu.at[j], ss, s_at("pgu", j, "r"), y_peer)
                else:
                    accgu[hs, cs] = res
            for e in range(2):
                es = slice(e * hid, (e + 1) * hid)
                res = dot(sht[es, :], gs[mb, k, :, hs])
                if not first:
                    res = res + accd[es, hs]
                if last and h == 1:
                    pd[e] = (res * scale).astype(BF)
                    ss = s_at("pd", "s")
                    rdma(pd.at[e], qd.at[e], ss, s_at("pd", e, "r"), y_peer)
                else:
                    accd[es, hs] = res

    def finish():
        for j, (ref, e) in enumerate([(dg_ref, 0), (dg_ref, 1), (du_ref, 0), (du_ref, 1)]):
            drain(qgu.at[j], s_at("pgu", j, "r"))
            outgu[j] = accgu[0:half, j * hid : (j + 1) * hid] * scale + qgu[j].astype(F32)
            pltpu.make_async_copy(outgu.at[j], ref.at[0, e], s_at("out")).start()
        for e in range(2):
            drain(qd.at[e], s_at("pd", e, "r"))
            outd[e] = accd[e * hid : (e + 1) * hid, 0:half] * scale + qd[e].astype(F32)
            pltpu.make_async_copy(outd.at[e], dd_ref.at[0, e], s_at("outd")).start()
        drain(outgu, s_at("out"))
        drain(outd, s_at("outd"))

    steps = dict(
        spread_meta=spread_meta, weights_gu=weights_gu, weights_d=weights_d, masks=masks,
        wait_gu=wait_gu, wait_d=wait_d, turn_x=turn_x,
        spread_x=spread_x, spread_g=spread_g, spread_last=spread_last, relay_last=relay_last,
        wait_x=wait_x, wait_g=wait_g, pre_gu=pre_gu, pre_d=pre_d, mid_gu=mid_gu, mid_d=mid_d,
        activate=activate, forward=forward, spread_acts=spread_acts, relay=relay,
        give_back=give_back, grads=grads, finish=finish,
    )
    for name, *where in schedule(n_ch):
        steps[name](*where)
    @pl.when(sec > 0)
    def _():
        drain(sent, s_at("shift", "s"))

    drain(bk, s_at("back", "r"))
    for tag, ref in (
        ("x", xs.at[:, :, pl.ds(0, rows - tk)]), ("g", gs.at[0, :, pl.ds(0, rows - tk)]),
        ("p1gu", p1gu), ("p1d", p1d), ("s2gu", s2gu), ("s2d", s2d),
        ("ag", act.at[:, :, pl.ds(0, 3 * tk)]), ("fw", act.at[:, :, pl.ds(0, four)]),
        ("back", bk.at[:, pl.ds(0, rows - tk)]), ("pgu", pgu), ("pd", pd),
    ):
        drain(ref, s_at(tag, "s"))

    drain(glq.at[pl.ds(0, tok - tok // 8)], s_at("last", "s"))

    @pl.when(sec < n_sec - 1)
    def _():
        drain(glq, s_at("lastq", "s"))

    for s, ref in sends:
        drain(ref, s)
    assert names.count == n_sems, names.count


def write_out(*refs):
    held, got, put = refs[8:12], refs[12], refs[13]
    parts = []
    for i in range(4):
        rows = refs[i].shape[-2] // 2
        for j in range(2):
            part = (Ellipsis, pl.ds(j * rows, rows), slice(None))
            n = 2 * i + j
            parts.append((
                pltpu.make_async_copy(refs[i].at[part], held[i].at[part], got.at[n]),
                pltpu.make_async_copy(held[i].at[part], refs[4 + i].at[part], put.at[n]),
            ))
    for first, _ in parts:
        first.start()
    for first, second in parts:
        first.wait()
        second.start()
    for _, second in parts:
        second.wait()


def body(tokens_in, grad_first, grad_last, expert_ids, gate_probs, w_gate, w_up, w_down):
    tok, width = tokens_in.shape[2:]
    half, hid = w_gate.shape[2:]
    wide = 2 * half
    tk = tok // CHUNKS
    rows, four = 2 * NX * tk, NX * tk
    n_sems = 22 + 20 * CHUNKS
    pair = (2, CHUNKS)
    scratch = [
        pltpu.VMEM(pair + (rows, wide), BF),
        pltpu.VMEM(pair + (rows, wide), BF),
        pltpu.VMEM((2 * NX * tok // 8, wide), BF),
        pltpu.VMEM((CHUNKS, rows, wide), BF),
        pltpu.VMEM((CHUNKS, rows, wide), BF),
        pltpu.VMEM((wide, 4 * hid), BF),
        pltpu.VMEM((2 * hid, wide), BF),
        pltpu.VMEM((2 * NX, 2, tok), jnp.int32),
        pltpu.VMEM(pair + (rows, 128), F32),
        pltpu.VMEM((2, tok, 128), F32),
        pltpu.VMEM(pair + (wide, rows), BF),
        pltpu.VMEM((2 * hid, rows), BF),
        pltpu.VMEM(pair + (rows, 3 * hid), BF),
        pltpu.VMEM(pair + (rows, 4 * hid), BF),
        pltpu.VMEM(pair + (rows, 2 * hid), BF),
    ]
    for cols in (2 * hid, hid):
        scratch += [
            pltpu.VMEM(pair + (four, cols), BF),
            pltpu.VMEM(pair + (four, cols), BF),
            pltpu.VMEM(pair + (four, cols), F32),
            pltpu.VMEM(pair + (NX - 1, tk, cols), BF),
            pltpu.VMEM(pair + (NX - 1, tk, cols), BF),
        ]
    scratch += [
        pltpu.VMEM((wide, 4 * hid), F32),
        pltpu.VMEM((2 * hid, wide), F32),
        pltpu.VMEM((4, half, hid), BF),
        pltpu.VMEM((2, hid, half), BF),
        pltpu.VMEM((4, half, hid), BF),
        pltpu.VMEM((2, hid, half), BF),
        pltpu.VMEM((4, half, hid), F32),
        pltpu.VMEM((2, hid, half), F32),
        pltpu.SemaphoreType.DMA((n_sems,)),
    ]
    vmem = pl.BlockSpec(memory_space=pltpu.VMEM)
    hbm = pl.BlockSpec(memory_space=pl.ANY)
    results = pl.pallas_call(
        functools.partial(kernel, (wide, half, hid), tok, n_sems),
        out_shape=(
            jax.ShapeDtypeStruct((1, tok, width), BF),
            jax.ShapeDtypeStruct(w_gate.shape, F32),
            jax.ShapeDtypeStruct(w_up.shape, F32),
            jax.ShapeDtypeStruct(w_down.shape, F32),
        ),
        in_specs=[hbm, hbm, hbm, vmem, vmem, hbm, hbm, hbm],
        out_specs=(hbm,) * 4,
        scratch_shapes=scratch,
        compiler_params=pltpu.CompilerParams(
            collective_id=0, has_side_effects=True, vmem_limit_bytes=60 << 20
        ),
        name="section",
    )(
        tokens_in, grad_first, grad_last, expert_ids.reshape(2, tok), gate_probs.reshape(2, tok),
        w_gate, w_up, w_down,
    )
    return pl.pallas_call(
        write_out,
        out_shape=tuple(jax.ShapeDtypeStruct(r.shape, r.dtype) for r in results),
        in_specs=[hbm] * 4,
        out_specs=(hbm,) * 4,
        scratch_shapes=[pltpu.VMEM(r.shape, r.dtype) for r in results]
        + [pltpu.SemaphoreType.DMA((8,))] * 2,
        name="write_out",
    )(*results)


def solution(mesh):
    placed = (
        P("pipe", None, "dp", None),
        P("pipe", "dp", None),
        P("dp", None),
        P("pipe", None, "dp", None),
        P("pipe", None, "dp"),
        P("pipe", None, "dp", None),
        P("pipe", None, "dp", None),
        P("pipe", None, None, "dp"),
    )
    return jax.shard_map(
        body,
        mesh=mesh,
        in_specs=placed,
        out_specs=(
            P("pipe", "dp", None),
            P("pipe", None, "dp", None),
            P("pipe", None, "dp", None),
            P("pipe", None, None, "dp"),
        ),
        check_vma=False,
    )
```
